256 devices in a mesh: row: 8 (over z), col: 16 (over x, y), rep: 2 (over core).
Axes of the slice: x: 4, y: 4, z: 8, core: 2. Of those that a mesh axis runs over, the one named last changes fastest.
Arguments:
- features: bfloat16 [65536, 256], P(('row', 'col', 'rep')), may hold values from -6 to 6
- tile_values: bfloat16 [8, 16, 2, 192, 128, 128], P('row', 'col', 'rep'), may hold values from -0.0546875 to 0.0546875
- tile_row: int32 [8, 16, 2, 192], P('row', 'col', 'rep'), may hold values from 0 to 63
- tile_col: int32 [8, 16, 2, 192], P('row', 'col', 'rep'), may hold values from 0 to 31
- tile_count: int32 [8, 16, 2], P('row', 'col', 'rep'), may hold values from 48 to 192, as said below
- weight: bfloat16 [256, 172], replicated, may hold values from -0.375 to 0.375
- labels: int32 [65536], P(('row', 'col', 'rep')), may hold values from 0 to 171
Outputs:
- logits: float32 [65536, 172], P(('row', 'col', 'rep'))
- grad_features: float32 [65536, 256], P(('row', 'col', 'rep'))
- grad_weight: float32 [256, 172], replicated
The draws below stay inside these ranges and needn't reach their ends.
Inputs may be any that keep to these rules, and one draw needn't show every extreme that they name: `tile_count`: slots at or beyond a device's count hold values that take no part. At least a quarter of every device's slots are live, and some device has all 192 live in every draw.
All inputs are finite; a program needn't handle non-finite values.
Results may differ from the reference program's by a relative error of at most 0.0095.
Values may be sent and summed in bfloat16 or wider, within the bound.
A program may use at most 128 MiB of HBM per device.

```python
import jax
import jax.numpy as jnp
from jax import lax

F = 256
C = 172
TILE = 128
SLOTS = 192
BLK_DEV = 2
ROW_BLOCKS = 64
COL_BLOCKS = 32
NODES = 65536
N_ROW = 8
N_COL = 16
N_REP = 2


def draw_tile_count(key, part):
    key = jax.random.fold_in(key, 11)
    first, second = jax.random.split(key)
    total = N_ROW * N_COL * N_REP
    counts = jax.random.randint(first, (total,), SLOTS // 4, SLOTS + 1)
    fullest = jax.random.randint(second, (), 0, total)
    counts = jnp.where(jnp.arange(total) == fullest, SLOTS, counts)
    return counts.reshape(N_ROW, N_COL, N_REP).astype(jnp.int32)


def with_ends(result, stream_key, low, high):
    shape = result.shape
    spot = [jax.random.randint(jax.random.fold_in(stream_key, axis), (), 0, shape[axis]) for axis in range(len(shape))]
    result = result.at[tuple(spot)].set(low)
    longest = shape.index(max(shape))
    spot[longest] = (spot[longest] + 1) % shape[longest]
    return result.at[tuple(spot)].set(high)


def levels(own_key, shape, shards, low, high):
    loudness, own = 1.0, jax.random.fold_in(own_key, 6)
    for axis_at, parts in shards:
        draws = jnp.exp(jax.random.uniform(jax.random.fold_in(own, axis_at), (parts,), jnp.float32, low / len(shards), high / len(shards)))
        loudness = loudness * jnp.repeat(draws, shape[axis_at] // parts).reshape([-1 if axis == axis_at else 1 for axis in range(len(shape))])
    return loudness


def scatter_about(rng, shape, spread, limit, cuts=(), kind=jnp.bfloat16):
    values = spread * jax.random.normal(rng, shape, jnp.float32)
    if cuts:
        values = values * levels(rng, shape, cuts, -0.22, 0.18)
    return jnp.clip(values, -limit, limit).astype(kind)


def setup_inputs(seed: int = 0) -> dict:
    streams_of = jax.random.split(jax.random.key(seed), 8)
    return {
        "features": scatter_about(streams_of[0], (NODES, F), 1.0, 6.0, ((0, 256),)),
        "tile_values": scatter_about(streams_of[1], (N_ROW, N_COL, N_REP, SLOTS, TILE, TILE), (SLOTS * TILE // BLK_DEV) ** -0.5, 0.0546875, ((0, 8), (1, 16), (2, 2))),
        "tile_row": with_ends(jax.random.randint(streams_of[2], (N_ROW, N_COL, N_REP, SLOTS), 0, ROW_BLOCKS), jax.random.fold_in(streams_of[2], 1), 0, ROW_BLOCKS - 1).astype(jnp.int32),
        "tile_col": with_ends(jax.random.randint(streams_of[3], (N_ROW, N_COL, N_REP, SLOTS), 0, COL_BLOCKS), jax.random.fold_in(streams_of[3], 1), 0, COL_BLOCKS - 1).astype(jnp.int32),
        "tile_count": draw_tile_count(jax.random.fold_in(streams_of[7], 71), 0),
        "weight": scatter_about(streams_of[5], (F, C), F ** -0.5, 0.375),
        "labels": with_ends(jax.random.randint(streams_of[6], (NODES,), 0, C), jax.random.fold_in(streams_of[6], 1), 0, C - 1).astype(jnp.int32),
    }


def propagate(values, take_ids, put_ids, live, source, out_blocks, backward):
    total = values.shape[0]
    tile = values.shape[-1]
    width = source.shape[-1]
    group = 256

    def step(acc, index):
        start = index * group
        part = lax.dynamic_slice_in_dim(values, start, group, 0).astype(jnp.float32)
        take = lax.dynamic_slice_in_dim(take_ids, start, group, 0)
        put = lax.dynamic_slice_in_dim(put_ids, start, group, 0)
        alive = lax.dynamic_slice_in_dim(live, start, group, 0)
        picked = source[take].astype(jnp.float32)
        if backward:
            prod = jnp.einsum("gji,gjw->giw", part, picked)
        else:
            prod = jnp.einsum("gij,gjw->giw", part, picked)
        prod = jnp.where(alive[:, None, None], prod, 0.0)
        return acc.at[put].add(prod), None

    start_acc = jnp.zeros((out_blocks, tile, width), jnp.float32)
    acc, _ = lax.scan(step, start_acc, jnp.arange(total // group, dtype=jnp.int32))
    return acc


def reference(features, tile_values, tile_row, tile_col, tile_count, weight, labels):
    tile = tile_values.shape[-1]
    blocks = NODES // tile
    rows_ix = jnp.arange(N_ROW, dtype=jnp.int32)[:, None, None, None]
    cols_ix = jnp.arange(N_COL, dtype=jnp.int32)[None, :, None, None]
    slot_ix = jnp.arange(SLOTS, dtype=jnp.int32)[None, None, None, :]
    row_global = rows_ix * ROW_BLOCKS + tile_row
    quot = tile_col // BLK_DEV
    col_global = ((quot // N_REP) * N_COL * N_REP + cols_ix * N_REP + quot % N_REP) * BLK_DEV + tile_col % BLK_DEV
    live = slot_ix < tile_count[..., None]
    values = tile_values.reshape(-1, tile, tile)
    row_flat = row_global.reshape(-1).astype(jnp.int32)
    col_flat = col_global.reshape(-1).astype(jnp.int32)
    live_flat = live.reshape(-1)
    source = features.reshape(blocks, tile, F)
    hidden = propagate(values, col_flat, row_flat, live_flat, source, blocks, False)
    hidden = hidden.reshape(NODES, F).astype(jnp.bfloat16)
    logits = jnp.dot(hidden, weight, preferred_element_type=jnp.float32)
    expos = jnp.exp(logits)
    prob = expos / jnp.sum(expos, axis=1, keepdims=True)
    onehot = (labels[:, None] == jnp.arange(C, dtype=jnp.int32)[None, :]).astype(jnp.float32)
    grad_logits = (prob - onehot).astype(jnp.bfloat16)
    grad_hidden = jnp.dot(grad_logits, weight.T, preferred_element_type=jnp.float32).astype(jnp.bfloat16)
    grad_weight = jnp.dot(hidden.T, grad_logits, preferred_element_type=jnp.float32)
    back = propagate(values, row_flat, col_flat, live_flat, grad_hidden.reshape(blocks, tile, F), blocks, True)
    grad_features = back.reshape(NODES, F)
    return logits, grad_features, grad_weight
```

```python
import functools

import jax
import jax.numpy as jnp
from jax import lax
from jax.experimental import pallas as pl
from jax.experimental.pallas import tpu as pltpu
from jax.sharding import PartitionSpec as P

BF = jnp.bfloat16
F32 = jnp.float32
VM = pltpu.VMEM
SIDE = 4
GROUP = 16
UNROLL = 4


class Link:
    def __init__(self, send, recv):
        self.send, self.recv, self.used, self.live = send, recv, 0, []

    def slot(self):
        self.used += 1
        return self.used - 1

    def start(self, src, dst, device, slot):
        copy = pltpu.make_async_remote_copy(
            src_ref=src,
            dst_ref=dst,
            send_sem=self.send.at[slot],
            recv_sem=self.recv.at[slot],
            device_id=device,
            device_id_type=pl.DeviceIdType.MESH,
        )
        copy.start()
        self.live.append(copy)

    def arrived(self, dst, slot):
        pltpu.make_async_remote_copy(
            src_ref=dst,
            dst_ref=dst,
            send_sem=self.send.at[slot],
            recv_sem=self.recv.at[slot],
            device_id={"rep": 1 - lax.axis_index("rep")},
            device_id_type=pl.DeviceIdType.MESH,
        ).wait_recv()

    def drain(self):
        for copy in self.live:
            copy.wait_send()


def enter(devices):
    barrier = pltpu.get_barrier_semaphore()
    for device in devices:
        pl.semaphore_signal(
            barrier, inc=1, device_id=device, device_id_type=pl.DeviceIdType.MESH
        )
    pl.semaphore_wait(barrier, len(devices))


def gather_z(feat, panel, send, recv):
    r, p = lax.axis_index("row"), lax.axis_index("rep")
    n = panel.shape[0]
    at = lambda k: lax.rem(r + k + 2 * n, n)
    right, left, twin = {"row": at(1)}, {"row": at(-1)}, {"rep": 1 - p}
    enter((right, left, twin))
    link = Link(send, recv)
    subs, rows = 2, feat.shape[0] // 2
    own = [feat.at[pl.ds(j * rows, rows)] for j in range(subs)]
    slot = {}
    for j in range(subs):
        for d, dev in ((1, right), (-1, left)):
            slot[1, d, j] = link.slot()
            link.start(own[j], panel.at[r, p, pl.ds(j * rows, rows)], dev, slot[1, d, j])
    slot["own"] = link.slot()
    link.start(feat, panel.at[r, p], twin, slot["own"])
    panel[r, p] = feat[...]
    twins = [(panel.at[r, 1 - p], slot["own"])]
    half = n // 2
    for k in range(1, half + 1):
        for j in range(subs):
            for d, dev in ((1, right), (-1, left)):
                if k == half and (j == 0) != (d == 1):
                    continue
                part = panel.at[at(-k * d), p, pl.ds(j * rows, rows)]
                link.arrived(part, slot[k, d, j])
                if k + 1 < half or (k + 1 == half and (j == 0) == (d == 1)):
                    slot[k + 1, d, j] = link.slot()
                    link.start(part, part, dev, slot[k + 1, d, j])
                extra = link.slot()
                link.start(part, part, twin, extra)
                twins.append((panel.at[at(-k * d), 1 - p, pl.ds(j * rows, rows)], extra))
    for part, extra in twins:
        link.arrived(part, extra)
    link.drain()


def tiles_kernel(backward, take_ids, put_ids, count, tiles, panel, out, acc):
    step = pl.program_id(0)
    base = step * GROUP
    live_count = count[0]

    @pl.when(step == 0)
    def _():
        acc[...] = jnp.zeros_like(acc)

    def body(turn, carry):
        for u in range(UNROLL):
            s = turn * UNROLL + u
            slot = base + s
            source = panel[take_ids[slot]]
            if backward:
                prod = lax.dot_general(
                    tiles[s], source, (((0,), (0,)), ((), ())), preferred_element_type=F32
                )
            else:
                prod = jnp.dot(tiles[s], source, preferred_element_type=F32)
            prod = jnp.where(slot < live_count, prod, 0.0)
            acc[put_ids[slot]] += prod
        return carry

    lax.fori_loop(0, GROUP // UNROLL, body, 0)

    @pl.when(step == pl.num_programs(0) - 1)
    def _():
        out[...] = acc[...].astype(out.dtype)


def multiply(backward, values, take_ids, put_ids, count, panel, blocks):
    slots, tile, _ = values.shape
    width = panel.shape[-1]
    return pl.pallas_call(
        functools.partial(tiles_kernel, backward),
        out_shape=jax.ShapeDtypeStruct((blocks, tile, width), BF),
        grid_spec=pltpu.PrefetchScalarGridSpec(
            num_scalar_prefetch=3,
            grid=(slots // GROUP,),
            in_specs=[
                pl.BlockSpec((GROUP, tile, tile), lambda i, *_: (i, 0, 0)),
                pl.BlockSpec(panel.shape, lambda i, *_: (0, 0, 0)),
            ],
            out_specs=pl.BlockSpec((blocks, tile, width), lambda i, *_: (0, 0, 0)),
            scratch_shapes=[VM((blocks, tile, width), F32)],
        ),
        compiler_params=pltpu.CompilerParams(vmem_limit_bytes=48 * 1024 * 1024),
    )(take_ids, put_ids, count, values, panel)


def add(a, b):
    return (a.astype(F32) + b.astype(F32)).astype(BF)


def plane_kernel(
    part, weight, labels, logits, panel, term,
    summed, far1, near1, mid, far2, near2, hidden, wpad, gw, gw1, gw2, send, recv,
):
    c, p = lax.axis_index("col"), lax.axis_index("rep")
    x, y = c // SIDE, lax.rem(c, SIDE)
    wrap = lambda v: lax.rem(v + 2 * SIDE, SIDE)
    twin = {"rep": 1 - p}
    pos = (x, y)

    def to(axis, k):
        if axis == 0:
            return {"col": wrap(x + k) * SIDE + y}
        return {"col": x * SIDE + wrap(y + k)}

    peers = [{"col": wrap(x + k) * SIDE + y, "rep": lax.rem(p + e, 2)}
             for k in range(SIDE) for e in range(2) if (k, e) != (0, 0)]
    mates = [to(1, k) for k in range(1, SIDE)]
    enter([*peers, *mates])
    link = Link(send, recv)
    rows = panel.shape[3]
    half = rows // 2
    cut = (pl.ds(0, half), pl.ds(half, half))

    def block(ref, h, a, b, *lead):
        if h == 0:
            return ref.at[(a, b, *lead, cut[0])]
        return ref.at[(b, a, *lead, cut[1])]

    whole, low, high = pl.ds(0, SIDE), pl.ds(0, SIDE // 2), pl.ds(SIDE // 2, SIDE // 2)
    order = [(h, k) for k in (2, 1, -1, 0) for h in (0, 1)]
    cores = {}
    for h, k in order:
        cores[h, k] = link.slot()
        a = wrap(pos[h] + k)
        link.start(block(part, h, a, whole, 1 - p), block(summed, h, a, whole), twin, cores[h, k])
    wpad[...] = jnp.zeros_like(wpad)
    classes = weight.shape[1]
    wpad[:, :classes] = weight[...]
    slots = {}

    def first(h, tag, src, dst, k):
        slots[h, tag] = link.slot()
        link.start(src, dst, to(h, k), slots[h, tag])

    for h, k in order:
        a = wrap(pos[h] + k)
        got = block(summed, h, a, whole)
        link.arrived(got, cores[h, k])
        got[...] = add(got[...], block(part, h, a, whole, p)[...])
        if k == 2:
            first(h, "A", block(summed, h, a, low), far1.at[h, 0], 1)
            first(h, "a", block(summed, h, a, high), far1.at[h, 1], -1)
        if k == 1:
            first(h, "B", block(summed, h, a, high), near1.at[h, 0, high], 1)
        if k == -1:
            first(h, "b", block(summed, h, a, low), near1.at[h, 1, low], -1)
            if h == 1:
                for g in (0, 1):
                    for side, tag, k2, span in ((0, "A", 1, low), (1, "a", -1, high)):
                        link.arrived(far1.at[g, side], slots[g, tag])
                        piece = block(summed, g, wrap(pos[g] + k2), span)
                        piece[...] = add(piece[...], far1[g, side])
                        first(g, "C" if side == 0 else "c", piece, near1.at[g, side, span], k2)
    quarter = half // 2
    lo, hi = pl.ds(0, quarter), pl.ds(quarter, quarter)

    def second(h, tag, src, dst, k):
        slots[h, tag] = link.slot()
        link.start(src, dst, to(1 - h, k), slots[h, tag])

    for h in (0, 1):
        link.arrived(near1.at[h, 0, high], slots[h, "B"])
        link.arrived(near1.at[h, 1, low], slots[h, "b"])
        link.arrived(near1.at[h, 0, low], slots[h, "C"])
        link.arrived(near1.at[h, 1, high], slots[h, "c"])
        mine = block(summed, h, pos[h], whole)
        mid[h] = (
            mine[...].astype(F32) + near1[h, 0].astype(F32) + near1[h, 1].astype(F32)
        ).astype(BF)
        o = pos[1 - h]
        second(h, "P", mid.at[h, wrap(o + 2), lo], far2.at[h, 0], 1)
        second(h, "p", mid.at[h, wrap(o + 2), hi], far2.at[h, 1], -1)
        second(h, "Q", mid.at[h, wrap(o + 1), hi], near2.at[h, 0, hi], 1)
        second(h, "q", mid.at[h, wrap(o - 1), lo], near2.at[h, 1, lo], -1)
    for h in (0, 1):
        o = pos[1 - h]
        for side, tag, k, span in ((0, "P", 1, lo), (1, "p", -1, hi)):
            link.arrived(far2.at[h, side], slots[h, tag])
            piece = mid.at[h, wrap(o + k), span]
            piece[...] = add(piece[...], far2[h, side])
            second(h, "R" if side == 0 else "r", piece, near2.at[h, side, span], k)
    nodes = labels.shape[1]
    lanes = wpad.shape[1]
    hot = (
        lax.broadcasted_iota(jnp.int32, (lanes, nodes), 0) == labels[...]
    ).astype(F32).T
    for h in (0, 1):
        link.arrived(near2.at[h, 0, hi], slots[h, "Q"])
        link.arrived(near2.at[h, 1, lo], slots[h, "q"])
        link.arrived(near2.at[h, 0, lo], slots[h, "R"])
        link.arrived(near2.at[h, 1, hi], slots[h, "r"])
        hidden[cut[h]] = (
            mid[h, pos[1 - h]].astype(F32) + near2[h, 0].astype(F32) + near2[h, 1].astype(F32)
        ).astype(BF)

    score = jnp.dot(hidden[...], wpad[...], preferred_element_type=F32)
    logits[...] = score[:, :classes]
    real = lax.broadcasted_iota(jnp.int32, score.shape, 1) < classes
    expos = jnp.where(real, jnp.exp(score), 0.0)
    prob = expos / jnp.sum(expos, axis=1, keepdims=True)
    grad = (prob - hot).astype(BF)
    panel[x, y, p] = lax.dot_general(
        grad, wpad[...], (((1,), (1,)), ((), ())), preferred_element_type=F32
    ).astype(BF)

    twins = []

    def hand(ref_mine, ref_twin):
        slot = link.slot()
        link.start(ref_mine, ref_mine, twin, slot)
        twins.append((ref_twin, slot))

    def spot(h, da, db, core, span=None):
        a, b = wrap(pos[h] + da), wrap(pos[1 - h] + db)
        i, j = (a, b) if h == 0 else (b, a)
        span = span if span is not None else cut[h]
        return panel.at[i, j, core, span]

    quarters = [(pl.ds(h * half, quarter), pl.ds(h * half + quarter, quarter)) for h in (0, 1)]

    def go(key, src, axis, k):
        slots[key] = link.slot()
        link.start(src, src, to(axis, k), slots[key])

    for h in (0, 1):
        own = spot(h, 0, 0, p)
        go((h, "g", 1), own, 1 - h, 1)
        go((h, "g", -1), own, 1 - h, -1)
    for h in (0, 1):
        own = spot(h, 0, 0, p)
        go((h, "s", 1, 0), own, h, 1)
        go((h, "s", -1, 0), own, h, -1)
        hand(own, spot(h, 0, 0, 1 - p))

    gw[...] = lax.dot_general(
        hidden[...], grad, (((0,), (0,)), ((), ())), preferred_element_type=F32
    )
    share = gw.shape[0] // (2 * SIDE)
    slot_w = []
    mine8 = x * 2 + p
    for k in range(SIDE):
        for e in range(2):
            if (k, e) == (0, 0):
                continue
            there = wrap(x + k) * 2 + lax.rem(p + e, 2)
            s = link.slot()
            link.start(gw.at[pl.ds(there * share, share)], gw1.at[mine8],
                       {"col": wrap(x + k) * SIDE + y, "rep": lax.rem(p + e, 2)}, s)
            slot_w.append((gw1.at[wrap(x - k) * 2 + lax.rem(p + e, 2)], s))

    for h in (0, 1):
        for d in (1, -1):
            got = spot(h, 0, -d, p)
            link.arrived(got, slots[h, "g", d])
            q = 0 if d == 1 else 1
            go((h, "f", d), spot(h, 0, -d, p, quarters[h][q]), 1 - h, d)
            go((h, "s", 1, -d), got, h, 1)
            go((h, "s", -1, -d), got, h, -1)
            hand(got, spot(h, 0, -d, 1 - p))

    gw1[mine8] = gw[pl.ds(mine8 * share, share)]
    for ref, s in slot_w:
        link.arrived(ref, s)
    total = gw1[0]
    for i in range(1, 2 * SIDE):
        total += gw1[i]
    gw[pl.ds(mine8 * share, share)] = total
    eighth = share // SIDE
    slot_w = []
    for k in range(1, SIDE):
        there = wrap(y + k)
        s = link.slot()
        link.start(gw.at[pl.ds(mine8 * share + there * eighth, eighth)], gw2.at[y], to(1, k), s)
        slot_w.append((gw2.at[wrap(y - k)], s))
    gw2[y] = gw[pl.ds(mine8 * share + y * eighth, eighth)]

    for h in (0, 1):
        for d in (1, -1):
            q = 0 if d == 1 else 1
            link.arrived(spot(h, 0, 2, p, quarters[h][q]), slots[h, "f", d])
        got = spot(h, 0, 2, p)
        go((h, "s", 1, 2), got, h, 1)
        go((h, "s", -1, 2), got, h, -1)
        hand(got, spot(h, 0, 2, 1 - p))
    for db in (0, 1, -1, 2):
        for h in (0, 1):
            for d in (1, -1):
                got = spot(h, -d, db, p)
                link.arrived(got, slots[h, "s", d, db])
                if (d == 1) == (db in (0, 1)):
                    go((h, "t", db), got, h, d)
                hand(got, spot(h, -d, db, 1 - p))
    for ref, s in slot_w:
        link.arrived(ref, s)
    term[...] = gw2[0] + gw2[1] + gw2[2] + gw2[3]
    for db in (0, 1, -1, 2):
        for h in (0, 1):
            got = spot(h, 2, db, p)
            link.arrived(got, slots[h, "t", db])
            hand(got, spot(h, 2, db, 1 - p))
    for ref, s in twins:
        link.arrived(ref, s)
    link.drain()


def scatter_z(part, term, out, gw, summed, inbox, wz, wfull, send, recv):
    r, c, p = lax.axis_index("row"), lax.axis_index("col"), lax.axis_index("rep")
    n = part.shape[0]
    x, y = c // SIDE, lax.rem(c, SIDE)
    wrap = lambda v: lax.rem(v + 2 * SIDE, SIDE)
    at = lambda k: lax.rem(r + k + 2 * n, n)
    right, left, twin = {"row": at(1)}, {"row": at(-1)}, {"rep": 1 - p}
    column = [{"row": at(k)} for k in range(1, n)]
    mates = [{"col": x * SIDE + wrap(y + k)} for k in range(1, SIDE)]
    peers = [{"col": wrap(x + k) * SIDE + y, "rep": lax.rem(p + e, 2)}
             for k in range(SIDE) for e in range(2) if (k, e) != (0, 0)]
    enter([*column, *mates, *peers])
    link = Link(send, recv)
    half = n // 2
    order = [half, *[s * k for k in range(half - 1, 0, -1) for s in (1, -1)], 0]
    cores = {}
    for k in order:
        cores[k] = link.slot()
        link.start(part.at[at(k), 1 - p], summed.at[at(k)], twin, cores[k])
    wait_w = []
    for k in range(1, n):
        s = link.slot()
        link.start(term, wz.at[r], {"row": at(k)}, s)
        wait_w.append((wz.at[at(-k)], s))
    wz[r] = term[...]

    def merge(k):
        link.arrived(summed.at[at(k)], cores[k])
        summed[at(k)] = add(summed[at(k)], part[at(k), p])

    subs = 4
    rows = summed.shape[1] // subs
    span = lambda j: pl.ds(j * rows, rows)
    slots = {}

    def go(k, d, j):
        dev = right if d == 1 else left
        slots[k, d, j] = link.slot()
        link.start(summed.at[at(k * d), span(j)], inbox.at[k - 1, (1 - d) // 2, span(j)], dev, slots[k, d, j])

    def far_part(d, j):
        return (j < subs // 2) == (d == 1)

    merge(half)
    for j in range(subs):
        for d in (1, -1):
            if far_part(d, j):
                go(half, d, j)
    eighth = term.shape[0]
    share = eighth * SIDE
    mine8 = x * 2 + p
    for k in range(half - 1, 0, -1):
        merge(k)
        merge(-k)
        for j in range(subs):
            for d in (1, -1):
                if k == half - 1 and not far_part(d, j):
                    go(k, d, j)
        for j in range(subs):
            for d in (1, -1):
                if k == half - 1 and not far_part(d, j):
                    continue
                link.arrived(inbox.at[k, (1 - d) // 2, span(j)], slots[k + 1, d, j])
                piece = summed.at[at(k * d), span(j)]
                piece[...] = add(piece[...], inbox[k, (1 - d) // 2, span(j)])
                go(k, d, j)
        if k == half - 1:
            for ref, s in wait_w:
                link.arrived(ref, s)
            total = wz[0]
            for i in range(1, n):
                total += wz[i]
            mine = wfull.at[pl.ds(mine8 * share + y * eighth, eighth)]
            mine[...] = total
            wait_w = []
            for k2 in range(1, SIDE):
                s = link.slot()
                link.start(mine, mine, {"col": x * SIDE + wrap(y + k2)}, s)
                wait_w.append((wfull.at[pl.ds(mine8 * share + wrap(y - k2) * eighth, eighth)], s))
        if k == half - 2:
            for ref, s in wait_w:
                link.arrived(ref, s)
            wait_w = []
            mine = wfull.at[pl.ds(mine8 * share, share)]
            for k2 in range(SIDE):
                for e in range(2):
                    if (k2, e) == (0, 0):
                        continue
                    core = lax.rem(p + e, 2)
                    s = link.slot()
                    link.start(mine, mine, {"col": wrap(x + k2) * SIDE + y, "rep": core}, s)
                    there = wrap(x - k2) * 2 + core
                    wait_w.append((wfull.at[pl.ds(there * share, share)], s))
    merge(0)
    for ref, s in wait_w:
        link.arrived(ref, s)
    gw[...] = wfull[:, : gw.shape[1]]
    for j in range(subs):
        for d in (1, -1):
            link.arrived(inbox.at[0, (1 - d) // 2, span(j)], slots[1, d, j])
        out[span(j)] = (
            summed[r, span(j)].astype(F32)
            + inbox[0, 0, span(j)].astype(F32)
            + inbox[0, 1, span(j)].astype(F32)
        )
    link.drain()


def call(kernel, outs, scratch, copies, number, *args):
    return pl.pallas_call(
        kernel,
        out_shape=[jax.ShapeDtypeStruct(s, t) for s, t in outs],
        in_specs=[pl.BlockSpec(memory_space=VM)] * len(args),
        out_specs=[pl.BlockSpec(memory_space=VM)] * len(outs),
        scratch_shapes=[
            *[VM(s, t) for s, t in scratch],
            pltpu.SemaphoreType.DMA((copies,)),
            pltpu.SemaphoreType.DMA((copies,)),
        ],
        compiler_params=pltpu.CompilerParams(
            collective_id=number, has_side_effects=True, vmem_limit_bytes=48 * 1024 * 1024
        ),
    )(*args)


def do_gather_z(features, n_row, n_rep):
    rows, width = features.shape
    return call(gather_z, [((n_row, n_rep, rows, width), BF)], [], 40, 0, features)[0]


def do_plane(part, weight, labels):
    side, _, _, rows, width = part.shape
    classes = weight.shape[1]
    lanes = 256
    half = rows // 2
    share = width // (2 * SIDE)
    return call(
        plane_kernel,
        [((rows, classes), F32), (part.shape, BF), ((share // SIDE, lanes), F32)],
        [
            ((side, side, rows, width), BF),
            ((2, 2, side // 2, half, width), BF),
            ((2, 2, side, half, width), BF),
            ((2, side, half, width), BF),
            ((2, 2, half // 2, width), BF),
            ((2, 2, half, width), BF),
            ((rows, width), BF),
            ((width, lanes), BF),
            ((width, lanes), F32),
            ((2 * SIDE, share, lanes), F32),
            ((SIDE, share // SIDE, lanes), F32),
        ],
        140,
        1,
        part,
        weight,
        labels,
    )


def do_scatter_z(part, term, classes):
    n, _, rows, width = part.shape
    lanes = term.shape[1]
    return call(
        scatter_z,
        [((rows, width), F32), ((width, classes), F32)],
        [
            ((n, rows, width), BF),
            ((n // 2, 2, rows, width), BF),
            ((n, *term.shape), F32),
            ((width, lanes), F32),
        ],
        90,
        2,
        part,
        term,
    )


def local(features, tile_values, tile_row, tile_col, tile_count, weight, labels):
    tile = tile_values.shape[-1]
    slots = tile_values.shape[3]
    rows, width = features.shape
    classes = weight.shape[1]
    n_row = lax.axis_size("row")
    n_col = lax.axis_size("col")
    n_rep = lax.axis_size("rep")
    row_blocks = n_col * n_rep * rows // tile
    col_blocks = n_row * n_rep * rows // tile
    values = tile_values.reshape(slots, tile, tile)
    block_rows = tile_row.reshape(slots)
    block_cols = tile_col.reshape(slots)
    count = tile_count.reshape(1)
    panel = do_gather_z(features, n_row, n_rep).reshape(col_blocks, tile, width)
    part = multiply(False, values, block_cols, block_rows, count, panel, row_blocks)
    part = part.reshape(SIDE, SIDE, n_rep, rows, width)
    logits, row_panel, term = do_plane(part, weight, labels.reshape(1, rows))
    row_panel = row_panel.reshape(row_blocks, tile, width)
    back = multiply(True, values, block_rows, block_cols, count, row_panel, col_blocks)
    back = back.reshape(n_row, n_rep, rows, width)
    grad_features, grad_weight = do_scatter_z(back, term, classes)
    return (logits, grad_features, grad_weight)


def solution(mesh):
    in_specs = (
        P(("row", "col", "rep"), None),
        P("row", "col", "rep", None, None, None),
        P("row", "col", "rep", None),
        P("row", "col", "rep", None),
        P("row", "col", "rep"),
        P(),
        P(("row", "col", "rep")),
    )
    out_specs = (P(("row", "col", "rep"), None), P(("row", "col", "rep"), None), P())
    return jax.shard_map(local, mesh=mesh, in_specs=in_specs, out_specs=out_specs, check_vma=False)
```
